32 devices in a mesh: slab: 8 (over y, x, core), pblk: 4 (over z).
Axes of the slice: x: 2, y: 2, z: 4, core: 2. Of those that a mesh axis runs over, the one named last changes fastest.
Arguments:
- gas_field: float32 [3, 512, 4096], P(None, 'slab', 'pblk'), may hold values from -6 to 6
- drift_field: float32 [2, 512, 4096], P(None, 'slab', 'pblk'), may hold values from 0.2 to 1
- particles: float32 [16384, 3, 128], P(('slab', 'pblk')), may hold values from -6 to 6
- coupling_rates: float32 [16384, 2, 128], P(('slab', 'pblk')), may hold values from 0.1 to 2
- block_owner: int32 [16384, 1], P(('slab', 'pblk')), may hold values from 0 to 31; in each aligned block of 512 rows (0 to 511, 512 to 1023, ...) at most 32 rows name the same one
- cell_index: int32 [16384, 128], P(('slab', 'pblk')), may hold values from 0 to 65535, as said below
- block_pairs: int32 [4096, 2], P(('slab', 'pblk')), may hold values from 0 to 511
- contact: int32 [4096, 128, 128], P(('slab', 'pblk')), may hold values 0 or 1
Outputs:
- gas_next: float32 [3, 512, 4096], P(None, 'slab', 'pblk')
- particles_next: float32 [16384, 3, 128], P(('slab', 'pblk'))
The draws below stay inside these ranges and needn't reach their ends.
Inputs may be any that keep to these rules, and one draw needn't show every extreme that they name: `block_owner`: of the rows of one device, at most 32 name the same owner, a bound that some block reaches. All particles of one block have the same cell_index // 128. `block_pairs`: both entries name blocks among the rows of the device that holds the pair.
All inputs are finite; a program needn't handle non-finite values. No bound on the sum of `contact` on one device may be relied on, other than what follows from the above.
Results may differ from the reference program's by a relative error of at most 0.000088.
Values sent between devices are 32-bit elements; how exact they have to be, the bound alone decides.
A program may use at most 64 MiB of HBM per device.

```python
import math
import jax
import jax.numpy as jnp
import numpy as np
from jax import lax

CX = 64
CW = 1024
BLOCK = 128
TILE = 128
NBLK_DEV = 512
NPAIR_DEV = 128
NX = 512
NW = 4096
NBLK = 16384
NPAIR = 4096
SLOTS = 32
N_SLAB = 8
N_PBLK = 4
DEVICES = 32


def draw_cell_index(key, part):
    tile_key = jax.random.fold_in(key, 11)
    offset_key = jax.random.fold_in(key, 23)
    tiles = jax.random.randint(tile_key, (NBLK, 1), 0, CX * CW // TILE)
    offsets = jax.random.randint(offset_key, (NBLK, BLOCK), 0, TILE)
    return (tiles * TILE + offsets).astype(jnp.int32)


def place_ends(values, own_key, low, high):
    longest = values.shape.index(max(values.shape))
    spots = []
    for shift in (0, 1):
        where = [jax.random.randint(jax.random.fold_in(own_key, axis), (), 0, length) for axis, length in enumerate(values.shape)]
        where[longest] = (where[longest] + shift) % values.shape[longest]
        spots.append(tuple(where))
    return values.at[spots[0]].set(low).at[spots[1]].set(high)


def levels(own_key, dims, split, smallest, top_value):
    def one(axis_at, shards_of):
        steps = jax.random.uniform(jax.random.fold_in(jax.random.fold_in(own_key, 6), axis_at), (shards_of,), jnp.float32, smallest / len(split), top_value / len(split))
        return jnp.repeat(jnp.exp(steps), dims[axis_at] // shards_of).reshape((-1,) + (1,) * (len(dims) - axis_at - 1))

    level = one(*split[0])
    for cut in split[1:]:
        level = level * one(*cut)
    return level


def assign_block(stream_key, own, number, rows, count, top, most, lean):
    order = jax.random.permutation(stream_key, count)
    heavy_load, ordinary = load_shares(count, rows * top, most, lean, True), load_shares(count, rows * top, most, lean, False)
    places = jnp.arange(count)

    def named(lengths, offset_by):
        used = int((lengths > 0).sum())
        fixed = max(1, used // 4)
        shifted = fixed + (places - fixed + offset_by * (used - fixed)) % max(1, count - fixed)
        return jnp.zeros((count,), jnp.int32).at[order[jnp.where(places < fixed, places, shifted)]].set(jnp.asarray(lengths, jnp.int32))

    lengths = jnp.where(number % 4 == 0, named(heavy_load, number // 4), named(ordinary, number - number // 4 - 1))
    mixed = jax.random.permutation(jax.random.fold_in(own, 3), count)
    source_of, sink = mixed[0:count // 2 * 2:2], mixed[1:count // 2 * 2:2]
    slack = jnp.minimum(lengths[source_of] - 1, most - lengths[sink]) // 2
    slack = jnp.where((source_of == order[0]) | (sink == order[0]) | (lengths[sink] == 0), 0, jnp.maximum(slack, 0))
    shifted = jax.random.randint(jax.random.fold_in(own, 4), (count // 2,), 0, 1 << 20) % (slack + 1)
    lengths = lengths.at[source_of].add(-shifted).at[sink].add(shifted)
    items = jnp.searchsorted(jnp.cumsum(lengths), jnp.arange(rows * top), side="right").astype(jnp.int32)
    table = items.reshape(top, rows).T
    table = table[jax.random.permutation(jax.random.fold_in(own, 1), rows)]
    offset_by = jax.random.randint(jax.random.fold_in(own, 2), (rows, 1), 0, top)
    return jnp.take_along_axis(table, (jnp.arange(top)[None, :] + offset_by) % top, axis=1)


def load_shares(amount, total, reach, lean, full):
    portions = [(1 << 20) // math.isqrt(grade ** lean) + 1 for grade in range(1, amount + 1)]
    largest = reach if full else min(reach, max(-(-total // amount), total * portions[0] // sum(portions)))
    least = 1 if total - largest >= amount - 1 else 0
    counts, spare = [largest] + [least] * (amount - 1), total - largest - least * (amount - 1)
    while spare > 0:
        candidates = [i for i in range(1, amount) if counts[i] < largest] or [i for i in range(1, amount) if counts[i] < reach]
        whole, remaining = sum([portions[i] for i in candidates]), spare
        for i in candidates:
            more = min(reach - counts[i], max(1, remaining * portions[i] // whole), spare)
            counts[i] = counts[i] + more
            spare = spare - more
    return np.array(counts)


def normal_values(rng, dims, width, limit, pieces=(), dtype=jnp.bfloat16):
    result = width * jax.random.normal(rng, dims, jnp.float32)
    if pieces:
        result = result * levels(rng, dims, pieces, -0.22, 0.18)
    return jnp.clip(result, -limit, limit).astype(dtype)


def setup_inputs(seed: int = 0) -> dict:
    keys = jax.random.split(jax.random.key(seed), 9)
    gas_field = normal_values(keys[0], (3, NX, NW), 1.0, 6.0, ((1, 8), (2, 4)), jnp.float32)
    drift_field = jnp.clip(0.2 + 0.8 * jax.random.uniform(keys[1], (2, NX, NW), jnp.float32) ** levels(keys[1], (2, NX, NW), ((1, 8), (2, 4)), -0.2, 0.2), 0.2, 1.0)
    particles = normal_values(keys[2], (NBLK, 3, BLOCK), 1.0, 6.0, ((0, 32),), jnp.float32)
    coupling_rates = jnp.clip(jnp.exp(math.log(2.0) - 2.9957323 * jax.random.uniform(keys[3], (NBLK, 2, BLOCK), jnp.float32) ** levels(keys[3], (NBLK, 2, BLOCK), ((0, 32),), -0.2, 0.2)), 0.1, 2.0)
    block_owner_keys = jax.random.split(jax.random.fold_in(keys[4], 1), NBLK // NBLK_DEV)
    block_owner_turns = jax.random.permutation(jax.random.fold_in(keys[4], 3), NBLK // NBLK_DEV)
    block_owner = jax.vmap(lambda own, number: assign_block(jax.random.fold_in(keys[4], 2), own, number, NBLK_DEV, DEVICES, 1, SLOTS, 2))(block_owner_keys, block_owner_turns).reshape((NBLK, 1))
    cell_index = draw_cell_index(jax.random.fold_in(keys[8], 71), 0)
    block_pairs = place_ends(jax.random.randint(keys[6], (NPAIR, 2), 0, NBLK_DEV), jax.random.fold_in(keys[6], 1), 0, NBLK_DEV - 1).astype(jnp.int32)
    contact = place_ends((jax.random.randint(keys[7], (NPAIR, BLOCK, BLOCK), 0, 8) < 1).astype(jnp.int32), jax.random.fold_in(keys[7], 1), 0, 1)
    return dict(gas_field=gas_field, drift_field=drift_field, particles=particles, coupling_rates=coupling_rates, block_owner=block_owner, cell_index=cell_index, block_pairs=block_pairs, contact=contact)


TIME_STEP = 0.2
VISCOSITY = 0.25
LOADING = 0.5
DAMPING = 0.1
CONDUCTION = 0.1


def tendency(padded, drift_center):
    middle = padded[:, 1:-1, 1:-1]
    west_cell = padded[:, :-2, 1:-1]
    east_cell = padded[:, 2:, 1:-1]
    south_cell = padded[:, 1:-1, :-2]
    north_cell = padded[:, 1:-1, 2:]
    upwind = drift_center[0] * (middle - west_cell) + drift_center[1] * (middle - south_cell)
    spread = west_cell + east_cell + south_cell + north_cell - 4.0 * middle
    return VISCOSITY * spread - upwind


def coupling_terms(gas_values, particle_state, rate_state):
    drag_force = rate_state[0] * (gas_values[0:2] - particle_state[0:2])
    heat_flow = rate_state[1] * (gas_values[2] - particle_state[2])
    return jnp.concatenate([drag_force, heat_flow[None]], axis=0)


def contact_terms(blocks, block_pairs, contact):
    first_block = blocks[block_pairs[:, 0]]
    second_block = blocks[block_pairs[:, 1]]
    weight = contact.astype(jnp.float32)
    into_first = jnp.einsum("pij,pcj->pci", weight, second_block, precision=lax.Precision.HIGHEST) - jnp.sum(weight, axis=2)[:, None, :] * first_block
    into_second = jnp.einsum("pij,pci->pcj", weight, first_block, precision=lax.Precision.HIGHEST) - jnp.sum(weight, axis=1)[:, None, :] * second_block
    summed = jnp.zeros_like(blocks).at[block_pairs[:, 0]].add(into_first).at[block_pairs[:, 1]].add(into_second)
    factor = jnp.array([DAMPING, DAMPING, CONDUCTION], jnp.float32)
    return summed * factor[None, :, None]


def reference(gas_field, drift_field, particles, coupling_rates, block_owner, cell_index, block_pairs, contact):
    widths = ((0, 0), (1, 1), (1, 1))
    section_one = gas_field + TIME_STEP * tendency(jnp.pad(gas_field, widths), drift_field)
    section_two = 0.5 * (gas_field + section_one + TIME_STEP * tendency(jnp.pad(section_one, widths), drift_field))
    device_count = N_SLAB * N_PBLK
    target = block_owner[:, 0]
    row_index = (target // N_PBLK)[:, None] * CX + cell_index // CW
    col_index = (target % N_PBLK)[:, None] * CW + cell_index % CW
    gas_values = section_two[:, row_index, col_index]
    particle_state = jnp.swapaxes(particles, 0, 1)
    exchange_terms = coupling_terms(gas_values, particle_state, jnp.swapaxes(coupling_rates, 0, 1))
    sources = jnp.zeros_like(section_two).at[:, row_index, col_index].add(exchange_terms)
    gas_next = section_two - TIME_STEP * LOADING * sources

    def per_device(device_item):
        return contact_terms(device_item[0], device_item[1], device_item[2])

    contact_force = lax.map(per_device, (particles.reshape(device_count, NBLK_DEV, 3, BLOCK), block_pairs.reshape(device_count, NPAIR_DEV, 2), contact.reshape(device_count, NPAIR_DEV, BLOCK, BLOCK)))
    contact_force = contact_force.reshape(NBLK, 3, BLOCK)
    particles_next = particles + TIME_STEP * (jnp.swapaxes(exchange_terms, 0, 1) + contact_force)
    return gas_next, particles_next
```

```python
import jax
import jax.numpy as jnp
from jax import lax
from jax.experimental import pallas as pl
from jax.experimental.pallas import tpu as pltpu
from jax.sharding import PartitionSpec as P

TIME_STEP = 0.2
VISCOSITY = 0.25
LOADING = 0.5
DAMPING = 0.1
LANES = 128
VMEM_BYTES = 48 * 1024 * 1024
BF = jnp.bfloat16
F32 = jnp.float32
NT = (((1,), (1,)), ((), ()))
NN = (((1,), (0,)), ((), ()))


def dot(a, b, dims=NN):
    return lax.dot_general(a, b, dims, preferred_element_type=F32)


def split(x):
    high = x.astype(BF)
    return high, (x - high.astype(F32)).astype(BF)


def select_rows(one_hot, values):
    high, low = split(values)
    return dot(one_hot, high) + dot(one_hot, low)


def tendency(v, xlo, xhi, wlo, whi, drift_x, drift_w):
    rows, cols = v.shape
    row = lax.broadcasted_iota(jnp.int32, v.shape, 0)
    col = lax.broadcasted_iota(jnp.int32, v.shape, 1)
    west = jnp.where(row == 0, xlo, pltpu.roll(v, 1, 0))
    east = jnp.where(row == rows - 1, xhi, pltpu.roll(v, rows - 1, 0))
    south = jnp.where(col == 0, wlo, pltpu.roll(v, 1, 1))
    north = jnp.where(col == cols - 1, whi, pltpu.roll(v, cols - 1, 1))
    upwind = drift_x * (v - west) + drift_w * (v - south)
    return VISCOSITY * (west + east + south + north - 4.0 * v) - upwind


def halo_terms(k, v, xlo, xhi, wlo, whi, drift):
    return tendency(
        v, xlo[k], xhi[k], wlo[k, :, LANES - 1 : LANES], whi[k, :, 0:1], drift[0], drift[1]
    )


def first_kernel(gas, drift, xlo, xhi, wlo, whi, out):
    for k in range(3):
        v = gas[k]
        out[k] = v + TIME_STEP * halo_terms(k, v, xlo, xhi, wlo, whi, drift)


def second_kernel(gas, one, drift, xlo, xhi, wlo, whi, tiles, out, sent, table):
    _, rows, cols = gas.shape
    per_row = cols // LANES
    for k in range(3):
        v = one[k]
        two = 0.5 * (gas[k] + v + TIME_STEP * halo_terms(k, v, xlo, xhi, wlo, whi, drift))
        out[k] = two
        for j in range(per_row):
            table[k, pl.ds(j, rows, stride=per_row), :] = two[:, j * LANES : (j + 1) * LANES]
    count = table.shape[1]
    slots = tiles.shape[0]
    one_hot = (
        tiles[...] == lax.broadcasted_iota(jnp.int32, (slots, count), 1)
    ).astype(F32).astype(BF)
    for k in range(3):
        sent[:, k * LANES : (k + 1) * LANES] = select_rows(one_hot, table[k])


def contact_kernel(pairs, particles, contact, acc, parts):
    step = pl.program_id(0)
    group = contact.shape[0]

    @pl.when(step == 0)
    def _():
        acc[...] = jnp.zeros_like(acc)
        parts[...] = jnp.ones_like(parts)
        for k in range(3):
            high, low = split(particles[:, k, :])
            parts[:, k, :] = high.astype(F32)
            parts[:, k + 3, :] = low.astype(F32)

    for r in range(group):
        at = (step * group + r) * 2
        a, b = pairs[at], pairs[at + 1]
        weight = contact[r].astype(F32).astype(BF)
        part_a, part_b = parts[a], parts[b]
        gain_a = dot(part_b.astype(BF), weight, NT)
        gain_b = dot(part_a.astype(BF), weight, NN)
        acc[a] = acc[a] + (gain_a - gain_a[6:7] * part_a)
        acc[b] = acc[b] + (gain_b - gain_b[6:7] * part_b)


def terms_kernel(got, slot_col, slot_row, cells, particles, rates, acc, sent, out, terms, spread):
    slots = got.shape[0]
    blocks = cells.shape[0]
    one_hot = (
        slot_col[...] == lax.broadcasted_iota(jnp.int32, (blocks, slots), 1)
    ).astype(F32).astype(BF)
    offsets = jnp.bitwise_and(cells[...], LANES - 1)
    for k in range(3):
        tile = select_rows(one_hot, got[:, k * LANES : (k + 1) * LANES])
        picked = jnp.take_along_axis(tile, offsets, axis=1)
        state = particles[:, k, :]
        term = rates[:, k // 2, :] * (picked - state)
        force = DAMPING * (acc[:, k, :] + acc[:, k + 3, :])
        out[:, k, :] = state + TIME_STEP * (term + force)
        high, low = split(term)
        terms[:, k, :] = high.astype(F32)
        terms[:, k + 3, :] = low.astype(F32)
    for k in (6, 7):
        terms[:, k, :] = jnp.zeros((blocks, LANES), F32)
    lane_of = lax.broadcasted_iota(jnp.int32, (LANES, LANES), 0)

    def one_group(step, carry):
        base = pl.multiple_of(step * 8, 8)
        near = jnp.bitwise_and(cells[pl.ds(base, 8), :], LANES - 1)
        for r in range(8):
            match = (near[r : r + 1] == lane_of).astype(F32).astype(BF)
            spread[base + r] = dot(terms[base + r].astype(BF), match, NT)
        return carry

    lax.fori_loop(0, blocks // 8, one_group, 0)
    into = (
        slot_row[...] == lax.broadcasted_iota(jnp.int32, (slots, blocks), 0)
    ).astype(F32).astype(BF)
    for k in range(3):
        summed = spread[:, k, :] + spread[:, k + 3, :]
        sent[:, k * LANES : (k + 1) * LANES] = select_rows(into, summed)


def sources_kernel(got, tiles, two, out, sums):
    _, rows, cols = two.shape
    per_row = cols // LANES
    slots = got.shape[0]
    count = sums.shape[1]
    one_hot = (
        tiles[...] == lax.broadcasted_iota(jnp.int32, (count, slots), 0)
    ).astype(F32).astype(BF)
    for k in range(3):
        sums[k] = select_rows(one_hot, got[:, k * LANES : (k + 1) * LANES])
        for j in range(per_row):
            cols_j = slice(j * LANES, (j + 1) * LANES)
            out[k, :, cols_j] = two[k, :, cols_j] - (TIME_STEP * LOADING) * sums[
                k, pl.ds(j, rows, stride=per_row), :
            ]


def params():
    return pltpu.CompilerParams(vmem_limit_bytes=VMEM_BYTES)


def cost(flops, moved):
    return pl.CostEstimate(flops=flops, bytes_accessed=moved, transcendentals=0)


def halos(v):
    found = []
    for axis, dim, width in (("slab", 1, 1), ("pblk", 2, LANES)):
        count = lax.axis_size(axis)
        up = [(i, i + 1) for i in range(count - 1)]
        down = [(i + 1, i) for i in range(count - 1)]
        size = v.shape[dim]
        found.append(lax.ppermute(lax.slice_in_dim(v, size - width, size, axis=dim), axis, up))
        found.append(lax.ppermute(lax.slice_in_dim(v, 0, width, axis=dim), axis, down))
    return found


def exchange(x):
    return lax.all_to_all(x, ("slab", "pblk"), split_axis=0, concat_axis=0, tiled=True)


def on_device(gas, drift, particles, rates, owner, cells, pairs, contact):
    devices = lax.axis_size("slab") * lax.axis_size("pblk")
    blocks = cells.shape[0]
    depth = max(2, 2 * blocks // devices)
    slots = devices * depth
    tile_count = gas.shape[1] * gas.shape[2] // LANES
    target = owner[:, 0]
    before = jnp.arange(blocks)[None, :] < jnp.arange(blocks)[:, None]
    same = target[None, :] == target[:, None]
    position = jnp.sum((before & same).astype(jnp.int32), axis=1)
    slot = target * depth + position
    tile = cells[:, 0] // LANES
    asked = jnp.sum(
        jnp.where(slot[None, :] == jnp.arange(slots)[:, None], tile[None, :], 0), axis=1
    ).reshape(devices, depth)
    tiles = exchange(asked).reshape(slots)

    field = jax.ShapeDtypeStruct(gas.shape, F32)
    wide = jax.ShapeDtypeStruct((slots, 3 * LANES), F32)
    one = pl.pallas_call(first_kernel, out_shape=field, compiler_params=params())(
        gas, drift, *halos(gas)
    )
    two, sent_gas = pl.pallas_call(
        second_kernel,
        out_shape=(field, wide),
        scratch_shapes=[pltpu.VMEM((3, tile_count, LANES), F32)],
        compiler_params=params(),
    )(gas, one, drift, *halos(one), tiles[:, None])
    got_gas = exchange(sent_gas)

    pair_count = contact.shape[0]
    group = 8
    acc = pl.pallas_call(
        contact_kernel,
        grid_spec=pltpu.PrefetchScalarGridSpec(
            num_scalar_prefetch=1,
            grid=(pair_count // group,),
            in_specs=[
                pl.BlockSpec(particles.shape, lambda i, s: (0, 0, 0)),
                pl.BlockSpec((group, LANES, LANES), lambda i, s: (i, 0, 0)),
            ],
            out_specs=pl.BlockSpec((blocks, 8, LANES), lambda i, s: (0, 0, 0)),
            scratch_shapes=[pltpu.VMEM((blocks, 8, LANES), F32)],
        ),
        out_shape=jax.ShapeDtypeStruct((blocks, 8, LANES), F32),
        compiler_params=params(),
        cost_estimate=cost(pair_count * 4 * 8 * LANES * LANES, 3 * contact.size * 4),
    )(pairs.reshape(-1), particles, contact)

    sent_terms, particles_next = pl.pallas_call(
        terms_kernel,
        out_shape=(wide, jax.ShapeDtypeStruct(particles.shape, F32)),
        scratch_shapes=[pltpu.VMEM((blocks, 8, LANES), F32)] * 2,
        compiler_params=params(),
    )(got_gas, slot[:, None], slot[None, :], cells, particles, rates, acc)
    gas_next = pl.pallas_call(
        sources_kernel,
        out_shape=field,
        scratch_shapes=[pltpu.VMEM((3, tile_count, LANES), F32)],
        compiler_params=params(),
    )(exchange(sent_terms), tiles[None, :], two)
    return gas_next, particles_next


def solution(mesh):
    own = ("slab", "pblk")
    grid = P(None, "slab", "pblk")
    in_specs = (
        grid,
        grid,
        P(own, None, None),
        P(own, None, None),
        P(own, None),
        P(own, None),
        P(own, None),
        P(own, None, None),
    )
    return jax.shard_map(
        on_device,
        mesh=mesh,
        in_specs=in_specs,
        out_specs=(grid, P(own, None, None)),
        check_vma=False,
    )
```

```python
import jax
import jax.numpy as jnp
from jax import lax
from jax.experimental import pallas as pl
from jax.experimental.pallas import tpu as pltpu
from jax.sharding import PartitionSpec as P

TIME_STEP = 0.2
VISCOSITY = 0.25
LOADING = 0.5
DAMPING = 0.1
LANES = 128
VMEM_BYTES = 48 * 1024 * 1024
BF = jnp.bfloat16
F32 = jnp.float32
NT = (((1,), (1,)), ((), ()))
NN = (((1,), (0,)), ((), ()))


def dot(a, b, dims=NN):
    return lax.dot_general(a, b, dims, preferred_element_type=F32)


def split(x):
    high = x.astype(BF)
    return high, (x - high.astype(F32)).astype(BF)


def select_rows(one_hot, values):
    high, low = split(values)
    return dot(one_hot, high) + dot(one_hot, low)


def tendency(v, xlo, xhi, wlo, whi, drift_x, drift_w):
    rows, cols = v.shape
    row = lax.broadcasted_iota(jnp.int32, v.shape, 0)
    col = lax.broadcasted_iota(jnp.int32, v.shape, 1)
    west = jnp.where(row == 0, xlo, pltpu.roll(v, 1, 0))
    east = jnp.where(row == rows - 1, xhi, pltpu.roll(v, rows - 1, 0))
    south = jnp.where(col == 0, wlo, pltpu.roll(v, 1, 1))
    north = jnp.where(col == cols - 1, whi, pltpu.roll(v, cols - 1, 1))
    upwind = drift_x * (v - west) + drift_w * (v - south)
    return VISCOSITY * (west + east + south + north - 4.0 * v) - upwind


def halo_terms(k, v, xlo, xhi, wlo, whi, drift):
    return tendency(
        v, xlo[k], xhi[k], wlo[k, :, LANES - 1 : LANES], whi[k, :, 0:1], drift[0], drift[1]
    )


def first_kernel(gas, drift, xlo, xhi, wlo, whi, out):
    for k in range(3):
        v = gas[k]
        out[k] = v + TIME_STEP * halo_terms(k, v, xlo, xhi, wlo, whi, drift)


def second_kernel(gas, one, drift, xlo, xhi, wlo, whi, tiles, out, sent, table):
    _, rows, cols = gas.shape
    per_row = cols // LANES
    for k in range(3):
        v = one[k]
        two = 0.5 * (gas[k] + v + TIME_STEP * halo_terms(k, v, xlo, xhi, wlo, whi, drift))
        out[k] = two
        for j in range(per_row):
            table[k, pl.ds(j, rows, stride=per_row), :] = two[:, j * LANES : (j + 1) * LANES]
    count = table.shape[1]
    slots = tiles.shape[0]
    one_hot = (
        tiles[...] == lax.broadcasted_iota(jnp.int32, (slots, count), 1)
    ).astype(F32).astype(BF)
    for k in range(3):
        sent[:, k * LANES : (k + 1) * LANES] = select_rows(one_hot, table[k])


def contact_kernel(pairs, particles, contact, acc, parts):
    step = pl.program_id(0)
    group = contact.shape[0]

    @pl.when(step == 0)
    def _():
        acc[...] = jnp.zeros_like(acc)
        parts[...] = jnp.ones_like(parts)
        for k in range(3):
            high, low = split(particles[:, k, :])
            parts[:, k, :] = high.astype(F32)
            parts[:, k + 3, :] = low.astype(F32)

    for r in range(group):
        at = (step * group + r) * 2
        a, b = pairs[at], pairs[at + 1]
        weight = contact[r].astype(F32).astype(BF)
        part_a, part_b = parts[a], parts[b]
        gain_a = dot(part_b.astype(BF), weight, NT)
        gain_b = dot(part_a.astype(BF), weight, NN)
        acc[a] = acc[a] + (gain_a - gain_a[6:7] * part_a)
        acc[b] = acc[b] + (gain_b - gain_b[6:7] * part_b)


def sums_kernel(slot_row, cells, particles, rates, rate_sums, state_sums, parts, spread):
    slots = rate_sums.shape[0]
    blocks = cells.shape[0]
    parts[...] = jnp.zeros_like(parts)
    for k in range(5):
        value = rates[:, k, :] if k < 2 else rates[:, (k - 2) // 2, :] * particles[:, k - 2, :]
        high, low = split(value)
        parts[:, k, :] = high.astype(F32)
        parts[:, k + 8, :] = low.astype(F32)
    lane_of = lax.broadcasted_iota(jnp.int32, (LANES, LANES), 0)

    def one_group(step, carry):
        base = pl.multiple_of(step * 8, 8)
        near = jnp.bitwise_and(cells[pl.ds(base, 8), :], LANES - 1)
        for r in range(8):
            match = (near[r : r + 1] == lane_of).astype(F32).astype(BF)
            summed = dot(parts[base + r].astype(BF), match, NT)
            spread[base + r] = summed[0:8] + summed[8:16]
        return carry

    lax.fori_loop(0, blocks // 8, one_group, 0)
    into = (
        slot_row[...] == lax.broadcasted_iota(jnp.int32, (slots, blocks), 0)
    ).astype(F32).astype(BF)
    for k in range(5):
        moved = select_rows(into, spread[:, k, :])
        if k == 0:
            rate_sums[:, 0:LANES] = moved
            rate_sums[:, LANES : 2 * LANES] = moved
        elif k == 1:
            rate_sums[:, 2 * LANES : 3 * LANES] = moved
        else:
            state_sums[:, (k - 2) * LANES : (k - 1) * LANES] = moved


def particles_kernel(got, slot_col, cells, particles, rates, acc, out):
    slots = got.shape[0]
    blocks = cells.shape[0]
    one_hot = (
        slot_col[...] == lax.broadcasted_iota(jnp.int32, (blocks, slots), 1)
    ).astype(F32).astype(BF)
    offsets = jnp.bitwise_and(cells[...], LANES - 1)
    for k in range(3):
        tile = select_rows(one_hot, got[:, k * LANES : (k + 1) * LANES])
        picked = jnp.take_along_axis(tile, offsets, axis=1)
        state = particles[:, k, :]
        term = rates[:, k // 2, :] * (picked - state)
        force = DAMPING * (acc[:, k, :] + acc[:, k + 3, :])
        out[:, k, :] = state + TIME_STEP * (term + force)


def sources_kernel(got, tiles, two, out, sums):
    _, rows, cols = two.shape
    per_row = cols // LANES
    slots = got.shape[0]
    count = sums.shape[1]
    one_hot = (
        tiles[...] == lax.broadcasted_iota(jnp.int32, (count, slots), 0)
    ).astype(F32).astype(BF)
    for k in range(3):
        sums[k] = select_rows(one_hot, got[:, k * LANES : (k + 1) * LANES])
        for j in range(per_row):
            cols_j = slice(j * LANES, (j + 1) * LANES)
            out[k, :, cols_j] = two[k, :, cols_j] - (TIME_STEP * LOADING) * sums[
                k, pl.ds(j, rows, stride=per_row), :
            ]


def params():
    return pltpu.CompilerParams(vmem_limit_bytes=VMEM_BYTES)


def cost(flops, moved):
    return pl.CostEstimate(flops=flops, bytes_accessed=moved, transcendentals=0)


def halos(v):
    found = []
    for axis, dim, width in (("slab", 1, 1), ("pblk", 2, LANES)):
        count = lax.axis_size(axis)
        up = [(i, i + 1) for i in range(count - 1)]
        down = [(i + 1, i) for i in range(count - 1)]
        size = v.shape[dim]
        found.append(lax.ppermute(lax.slice_in_dim(v, size - width, size, axis=dim), axis, up))
        found.append(lax.ppermute(lax.slice_in_dim(v, 0, width, axis=dim), axis, down))
    return found


def exchange(x):
    return lax.all_to_all(x, ("slab", "pblk"), split_axis=0, concat_axis=0, tiled=True)


def on_device(gas, drift, particles, rates, owner, cells, pairs, contact):
    devices = lax.axis_size("slab") * lax.axis_size("pblk")
    blocks = cells.shape[0]
    depth = max(2, 2 * blocks // devices)
    slots = devices * depth
    tile_count = gas.shape[1] * gas.shape[2] // LANES
    target = owner[:, 0]
    before = jnp.arange(blocks)[None, :] < jnp.arange(blocks)[:, None]
    same = target[None, :] == target[:, None]
    position = jnp.sum((before & same).astype(jnp.int32), axis=1)
    slot = target * depth + position
    tile = cells[:, 0] // LANES
    asked = jnp.sum(
        jnp.where(slot[None, :] == jnp.arange(slots)[:, None], tile[None, :], 0), axis=1
    ).reshape(devices, depth)
    tiles = exchange(asked).reshape(slots)

    field = jax.ShapeDtypeStruct(gas.shape, F32)
    wide = jax.ShapeDtypeStruct((slots, 3 * LANES), F32)
    one = pl.pallas_call(first_kernel, out_shape=field, compiler_params=params())(
        gas, drift, *halos(gas)
    )
    two, sent_gas = pl.pallas_call(
        second_kernel,
        out_shape=(field, wide),
        scratch_shapes=[pltpu.VMEM((3, tile_count, LANES), F32)],
        compiler_params=params(),
    )(gas, one, drift, *halos(one), tiles[:, None])
    slot_row, sent_gas = lax.optimization_barrier((slot[None, :], sent_gas))
    rate_sums, state_sums = pl.pallas_call(
        sums_kernel,
        out_shape=(wide, wide),
        scratch_shapes=[pltpu.VMEM((blocks, 16, LANES), F32), pltpu.VMEM((blocks, 8, LANES), F32)],
        compiler_params=params(),
        cost_estimate=cost(blocks * 32 * LANES * LANES, 80_000_000),
    )(slot_row, cells, particles, rates)
    got_gas = exchange(sent_gas)
    sent_terms = got_gas * rate_sums - state_sums
    pairs, sent_terms = lax.optimization_barrier((pairs, sent_terms))
    got_terms = exchange(sent_terms)

    pair_count = contact.shape[0]
    group = 8
    acc = pl.pallas_call(
        contact_kernel,
        grid_spec=pltpu.PrefetchScalarGridSpec(
            num_scalar_prefetch=1,
            grid=(pair_count // group,),
            in_specs=[
                pl.BlockSpec(particles.shape, lambda i, s: (0, 0, 0)),
                pl.BlockSpec((group, LANES, LANES), lambda i, s: (i, 0, 0)),
            ],
            out_specs=pl.BlockSpec((blocks, 8, LANES), lambda i, s: (0, 0, 0)),
            scratch_shapes=[pltpu.VMEM((blocks, 8, LANES), F32)],
        ),
        out_shape=jax.ShapeDtypeStruct((blocks, 8, LANES), F32),
        compiler_params=params(),
        cost_estimate=cost(pair_count * 4 * 8 * LANES * LANES, 3 * contact.size * 4),
    )(pairs.reshape(-1), particles, contact)

    particles_next = pl.pallas_call(
        particles_kernel,
        out_shape=jax.ShapeDtypeStruct(particles.shape, F32),
        compiler_params=params(),
        cost_estimate=cost(blocks * slots * 12 * LANES, 10_000_000),
    )(got_gas, slot[:, None], cells, particles, rates, acc)
    gas_next = pl.pallas_call(
        sources_kernel,
        out_shape=field,
        scratch_shapes=[pltpu.VMEM((3, tile_count, LANES), F32)],
        compiler_params=params(),
    )(got_terms, tiles[None, :], two)
    return gas_next, particles_next


def solution(mesh):
    own = ("slab", "pblk")
    grid = P(None, "slab", "pblk")
    in_specs = (
        grid,
        grid,
        P(own, None, None),
        P(own, None, None),
        P(own, None),
        P(own, None),
        P(own, None),
        P(own, None, None),
    )
    return jax.shard_map(
        on_device,
        mesh=mesh,
        in_specs=in_specs,
        out_specs=(grid, P(own, None, None)),
        check_vma=False,
    )
```

```python
import jax
import jax.numpy as jnp
from jax import lax
from jax.experimental import pallas as pl
from jax.experimental.pallas import tpu as pltpu
from jax.sharding import PartitionSpec as P

TIME_STEP = 0.2
VISCOSITY = 0.25
LOADING = 0.5
DAMPING = 0.1
LANES = 128
VMEM_BYTES = 48 * 1024 * 1024
BF = jnp.bfloat16
F32 = jnp.float32
NT = (((1,), (1,)), ((), ()))
NN = (((1,), (0,)), ((), ()))


def dot(a, b, dims=NN):
    return lax.dot_general(a, b, dims, preferred_element_type=F32)


def split(x):
    high = x.astype(BF)
    return high, (x - high.astype(F32)).astype(BF)


def select_rows(one_hot, values):
    high, low = split(values)
    return dot(one_hot, high) + dot(one_hot, low)


def tendency(v, xlo, xhi, wlo, whi, drift_x, drift_w):
    rows, cols = v.shape
    row = lax.broadcasted_iota(jnp.int32, v.shape, 0)
    col = lax.broadcasted_iota(jnp.int32, v.shape, 1)
    west = jnp.where(row == 0, xlo, pltpu.roll(v, 1, 0))
    east = jnp.where(row == rows - 1, xhi, pltpu.roll(v, rows - 1, 0))
    south = jnp.where(col == 0, wlo, pltpu.roll(v, 1, 1))
    north = jnp.where(col == cols - 1, whi, pltpu.roll(v, cols - 1, 1))
    upwind = drift_x * (v - west) + drift_w * (v - south)
    return VISCOSITY * (west + east + south + north - 4.0 * v) - upwind


def transport_kernel(gas, drift, out, table, one, rows_in, cols_in, send, recv):
    _, rows, cols = gas.shape
    per_row = cols // LANES
    x, w = lax.axis_index("slab"), lax.axis_index("pblk")
    nx, nw = lax.axis_size("slab"), lax.axis_size("pblk")
    places = (
        (lax.rem(x + 1, nx), w),
        (lax.rem(x + nx - 1, nx), w),
        (x, lax.rem(w + 1, nw)),
        (x, lax.rem(w + nw - 1, nw)),
    )
    barrier = pltpu.get_barrier_semaphore()
    for place in places:
        pl.semaphore_signal(
            barrier, inc=1, device_id=place, device_id_type=pl.DeviceIdType.MESH
        )
    pl.semaphore_wait(barrier, 4)

    def trade(v, turn):
        edges = (
            (v.at[:, pl.ds(rows - 8, 8), :], rows_in.at[2 * turn]),
            (v.at[:, pl.ds(0, 8), :], rows_in.at[2 * turn + 1]),
            (v.at[:, :, pl.ds(cols - LANES, LANES)], cols_in.at[2 * turn]),
            (v.at[:, :, pl.ds(0, LANES)], cols_in.at[2 * turn + 1]),
        )
        copies = [
            pltpu.make_async_remote_copy(
                src_ref=src,
                dst_ref=dst,
                send_sem=send.at[4 * turn + n],
                recv_sem=recv.at[4 * turn + n],
                device_id=places[n],
                device_id_type=pl.DeviceIdType.MESH,
            )
            for n, (src, dst) in enumerate(edges)
        ]
        for copy in copies:
            copy.start()
        return copies

    def stencil(v, k, turn):
        xlo = jnp.where(x == 0, 0.0, rows_in[2 * turn, k, 7:8, :])
        xhi = jnp.where(x == nx - 1, 0.0, rows_in[2 * turn + 1, k, 0:1, :])
        wlo = jnp.where(w == 0, 0.0, cols_in[2 * turn, k][:, LANES - 1 : LANES])
        whi = jnp.where(w == nw - 1, 0.0, cols_in[2 * turn + 1, k][:, 0:1])
        return tendency(v, xlo, xhi, wlo, whi, drift[0], drift[1])

    copies = trade(gas, 0)
    for copy in copies:
        copy.wait()
    for k in range(3):
        v = gas[k]
        one[k] = v + TIME_STEP * stencil(v, k, 0)
    copies = trade(one, 1)
    for copy in copies:
        copy.wait()
    for k in range(3):
        v = one[k]
        two = 0.5 * (gas[k] + v + TIME_STEP * stencil(v, k, 1))
        out[k] = two
        for j in range(per_row):
            table[k, pl.ds(j, rows, stride=per_row), :] = two[:, j * LANES : (j + 1) * LANES]


def gather_kernel(table, tiles, sent):
    count = table.shape[1]
    slots = tiles.shape[0]
    one_hot = (
        tiles[...] == lax.broadcasted_iota(jnp.int32, (slots, count), 1)
    ).astype(F32).astype(BF)
    for k in range(3):
        sent[:, k * LANES : (k + 1) * LANES] = select_rows(one_hot, table[k])


def combine_kernel(got, rate_sums, state_sums, sent):
    sent[...] = got[...] * rate_sums[...] - state_sums[...]


def contact_kernel(pairs, particles, contact, acc, parts):
    step = pl.program_id(0)
    group = contact.shape[0]

    @pl.when(step == 0)
    def _():
        acc[...] = jnp.zeros_like(acc)
        parts[...] = jnp.ones_like(parts)
        for k in range(3):
            high, low = split(particles[:, k, :])
            parts[:, k, :] = high.astype(F32)
            parts[:, k + 3, :] = low.astype(F32)

    for r in range(group):
        at = (step * group + r) * 2
        a, b = pairs[at], pairs[at + 1]
        weight = contact[r].astype(F32).astype(BF)
        part_a, part_b = parts[a], parts[b]
        gain_a = dot(part_b.astype(BF), weight, NT)
        gain_b = dot(part_a.astype(BF), weight, NN)
        acc[a] = acc[a] + (gain_a - gain_a[6:7] * part_a)
        acc[b] = acc[b] + (gain_b - gain_b[6:7] * part_b)


def sums_kernel(slot_row, cells, particles, rates, rate_sums, state_sums, parts, spread):
    slots = rate_sums.shape[0]
    blocks = cells.shape[0]
    parts[...] = jnp.zeros_like(parts)
    for k in range(5):
        value = rates[:, k, :] if k < 2 else rates[:, (k - 2) // 2, :] * particles[:, k - 2, :]
        high, low = split(value)
        parts[:, k, :] = high.astype(F32)
        parts[:, k + 8, :] = low.astype(F32)
    lane_of = lax.broadcasted_iota(jnp.int32, (LANES, LANES), 0)

    def one_group(step, carry):
        base = pl.multiple_of(step * 8, 8)
        near = jnp.bitwise_and(cells[pl.ds(base, 8), :], LANES - 1)
        for r in range(8):
            match = (near[r : r + 1] == lane_of).astype(F32).astype(BF)
            summed = dot(parts[base + r].astype(BF), match, NT)
            spread[base + r] = summed[0:8] + summed[8:16]
        return carry

    lax.fori_loop(0, blocks // 8, one_group, 0)
    into = (
        slot_row[...] == lax.broadcasted_iota(jnp.int32, (slots, blocks), 0)
    ).astype(F32).astype(BF)
    for k in range(5):
        moved = select_rows(into, spread[:, k, :])
        if k == 0:
            rate_sums[:, 0:LANES] = moved
            rate_sums[:, LANES : 2 * LANES] = moved
        elif k == 1:
            rate_sums[:, 2 * LANES : 3 * LANES] = moved
        else:
            state_sums[:, (k - 2) * LANES : (k - 1) * LANES] = moved


def particles_kernel(got, slot_col, cells, particles, rates, acc, out):
    slots = got.shape[0]
    blocks = cells.shape[0]
    one_hot = (
        slot_col[...] == lax.broadcasted_iota(jnp.int32, (blocks, slots), 1)
    ).astype(F32).astype(BF)
    offsets = jnp.bitwise_and(cells[...], LANES - 1)
    for k in range(3):
        tile = select_rows(one_hot, got[:, k * LANES : (k + 1) * LANES])
        picked = jnp.take_along_axis(tile, offsets, axis=1)
        state = particles[:, k, :]
        term = rates[:, k // 2, :] * (picked - state)
        force = DAMPING * (acc[:, k, :] + acc[:, k + 3, :])
        out[:, k, :] = state + TIME_STEP * (term + force)


def sources_kernel(got, tiles, two, out, sums):
    _, rows, cols = two.shape
    per_row = cols // LANES
    slots = got.shape[0]
    count = sums.shape[1]
    one_hot = (
        tiles[...] == lax.broadcasted_iota(jnp.int32, (count, slots), 0)
    ).astype(F32).astype(BF)
    for k in range(3):
        sums[k] = select_rows(one_hot, got[:, k * LANES : (k + 1) * LANES])
        for j in range(per_row):
            cols_j = slice(j * LANES, (j + 1) * LANES)
            out[k, :, cols_j] = two[k, :, cols_j] - (TIME_STEP * LOADING) * sums[
                k, pl.ds(j, rows, stride=per_row), :
            ]


def params():
    return pltpu.CompilerParams(vmem_limit_bytes=VMEM_BYTES)


def cost(flops, moved):
    return pl.CostEstimate(flops=flops, bytes_accessed=moved, transcendentals=0)


def exchange(x):
    return lax.all_to_all(x, ("slab", "pblk"), split_axis=0, concat_axis=0, tiled=True)


def on_device(gas, drift, particles, rates, owner, cells, pairs, contact):
    devices = lax.axis_size("slab") * lax.axis_size("pblk")
    blocks = cells.shape[0]
    depth = max(2, 2 * blocks // devices)
    slots = devices * depth
    tile_count = gas.shape[1] * gas.shape[2] // LANES
    target = owner[:, 0]
    before = jnp.arange(blocks)[None, :] < jnp.arange(blocks)[:, None]
    same = target[None, :] == target[:, None]
    position = jnp.sum((before & same).astype(jnp.int32), axis=1)
    slot = target * depth + position
    tile = cells[:, 0] // LANES
    asked = jnp.sum(
        jnp.where(slot[None, :] == jnp.arange(slots)[:, None], tile[None, :], 0), axis=1
    ).reshape(devices, depth)
    tiles = exchange(asked).reshape(slots)

    field = jax.ShapeDtypeStruct(gas.shape, F32)
    wide = jax.ShapeDtypeStruct((slots, 3 * LANES), F32)
    rows, cols = gas.shape[1:]
    two, table = pl.pallas_call(
        transport_kernel,
        out_shape=(field, jax.ShapeDtypeStruct((3, tile_count, LANES), F32)),
        in_specs=[pl.BlockSpec(memory_space=pltpu.VMEM)] * 2,
        out_specs=(pl.BlockSpec(memory_space=pltpu.VMEM),) * 2,
        scratch_shapes=[
            pltpu.VMEM((3, rows, cols), F32),
            pltpu.VMEM((4, 3, 8, cols), F32),
            pltpu.VMEM((4, 3, rows, LANES), F32),
            pltpu.SemaphoreType.DMA((8,)),
            pltpu.SemaphoreType.DMA((8,)),
        ],
        compiler_params=pltpu.CompilerParams(
            collective_id=0, has_side_effects=True, vmem_limit_bytes=VMEM_BYTES
        ),
        cost_estimate=cost(3 * 40 * rows * cols, 30_000_000),
    )(gas, drift)
    sent_gas = pl.pallas_call(gather_kernel, out_shape=wide, compiler_params=params())(
        table, tiles[:, None]
    )
    slot_row, sent_gas = lax.optimization_barrier((slot[None, :], sent_gas))
    rate_sums, state_sums = pl.pallas_call(
        sums_kernel,
        out_shape=(wide, wide),
        scratch_shapes=[pltpu.VMEM((blocks, 16, LANES), F32), pltpu.VMEM((blocks, 8, LANES), F32)],
        compiler_params=params(),
        cost_estimate=cost(blocks * 32 * LANES * LANES, 80_000_000),
    )(slot_row, cells, particles, rates)
    got_gas = exchange(sent_gas)
    sent_terms = pl.pallas_call(combine_kernel, out_shape=wide, compiler_params=params())(
        got_gas, rate_sums, state_sums
    )
    pairs, sent_terms = lax.optimization_barrier((pairs, sent_terms))
    got_terms = exchange(sent_terms)

    pair_count = contact.shape[0]
    group = 8
    acc = pl.pallas_call(
        contact_kernel,
        grid_spec=pltpu.PrefetchScalarGridSpec(
            num_scalar_prefetch=1,
            grid=(pair_count // group,),
            in_specs=[
                pl.BlockSpec(particles.shape, lambda i, s: (0, 0, 0)),
                pl.BlockSpec((group, LANES, LANES), lambda i, s: (i, 0, 0)),
            ],
            out_specs=pl.BlockSpec((blocks, 8, LANES), lambda i, s: (0, 0, 0)),
            scratch_shapes=[pltpu.VMEM((blocks, 8, LANES), F32)],
        ),
        out_shape=jax.ShapeDtypeStruct((blocks, 8, LANES), F32),
        compiler_params=params(),
        cost_estimate=cost(pair_count * 4 * 8 * LANES * LANES, 3 * contact.size * 4),
    )(pairs.reshape(-1), particles, contact)

    particles_next = pl.pallas_call(
        particles_kernel,
        out_shape=jax.ShapeDtypeStruct(particles.shape, F32),
        compiler_params=params(),
        cost_estimate=cost(blocks * slots * 12 * LANES, 10_000_000),
    )(got_gas, slot[:, None], cells, particles, rates, acc)
    gas_next = pl.pallas_call(
        sources_kernel,
        out_shape=field,
        scratch_shapes=[pltpu.VMEM((3, tile_count, LANES), F32)],
        compiler_params=params(),
    )(got_terms, tiles[None, :], two)
    return gas_next, particles_next


def solution(mesh):
    own = ("slab", "pblk")
    grid = P(None, "slab", "pblk")
    in_specs = (
        grid,
        grid,
        P(own, None, None),
        P(own, None, None),
        P(own, None),
        P(own, None),
        P(own, None),
        P(own, None, None),
    )
    return jax.shard_map(
        on_device,
        mesh=mesh,
        in_specs=in_specs,
        out_specs=(grid, P(own, None, None)),
        check_vma=False,
    )
```

```python
import jax
import jax.numpy as jnp
from jax import lax
from jax.experimental import pallas as pl
from jax.experimental.pallas import tpu as pltpu
from jax.sharding import PartitionSpec as P

TIME_STEP = 0.2
VISCOSITY = 0.25
LOADING = 0.5
DAMPING = 0.1
LANES = 128
VMEM_BYTES = 48 * 1024 * 1024
BF = jnp.bfloat16
F32 = jnp.float32
NT = (((1,), (1,)), ((), ()))
NN = (((1,), (0,)), ((), ()))


def dot(a, b, dims=NN):
    return lax.dot_general(a, b, dims, preferred_element_type=F32)


def split(x):
    high = x.astype(BF)
    return high, (x - high.astype(F32)).astype(BF)


def select_rows(one_hot, values):
    high, low = split(values)
    return dot(one_hot, high) + dot(one_hot, low)


def tendency(v, xlo, xhi, wlo, whi, drift_x, drift_w):
    rows, cols = v.shape
    row = lax.broadcasted_iota(jnp.int32, v.shape, 0)
    col = lax.broadcasted_iota(jnp.int32, v.shape, 1)
    west = jnp.where(row == 0, xlo, pltpu.roll(v, 1, 0))
    east = jnp.where(row == rows - 1, xhi, pltpu.roll(v, rows - 1, 0))
    south = jnp.where(col == 0, wlo, pltpu.roll(v, 1, 1))
    north = jnp.where(col == cols - 1, whi, pltpu.roll(v, cols - 1, 1))
    upwind = drift_x * (v - west) + drift_w * (v - south)
    return VISCOSITY * (west + east + south + north - 4.0 * v) - upwind


def transport_kernel(
    gas, drift, out, table, one, rows_out, cols_out, rows_in, cols_in, send, recv
):
    _, rows, cols = gas.shape
    per_row = cols // LANES
    x, w = lax.axis_index("slab"), lax.axis_index("pblk")
    nx, nw = lax.axis_size("slab"), lax.axis_size("pblk")
    places = (
        (lax.rem(x + 1, nx), w),
        (lax.rem(x + nx - 1, nx), w),
        (x, lax.rem(w + 1, nw)),
        (x, lax.rem(w + nw - 1, nw)),
    )
    barrier = pltpu.get_barrier_semaphore()
    for place in places:
        pl.semaphore_signal(
            barrier, inc=1, device_id=place, device_id_type=pl.DeviceIdType.MESH
        )
    rows_out[...] = jnp.zeros_like(rows_out)
    cols_out[...] = jnp.zeros_like(cols_out)

    def pack(v, k, turn):
        rows_out[2 * turn, k : k + 1, :] = v[rows - 1 : rows, :]
        rows_out[2 * turn + 1, k : k + 1, :] = v[0:1, :]
        cols_out[2 * turn, :, k : k + 1] = v[:, cols - 1 : cols]
        cols_out[2 * turn + 1, :, k : k + 1] = v[:, 0:1]

    for k in range(3):
        pack(gas[k], k, 0)
    pl.semaphore_wait(barrier, 4)

    def trade(turn):
        low, high = 2 * turn, 2 * turn + 1
        edges = (
            (rows_out.at[low], rows_in.at[low]),
            (rows_out.at[high], rows_in.at[high]),
            (cols_out.at[low], cols_in.at[low]),
            (cols_out.at[high], cols_in.at[high]),
        )
        copies = [
            pltpu.make_async_remote_copy(
                src_ref=src,
                dst_ref=dst,
                send_sem=send.at[4 * turn + n],
                recv_sem=recv.at[4 * turn + n],
                device_id=places[n],
                device_id_type=pl.DeviceIdType.MESH,
            )
            for n, (src, dst) in enumerate(edges)
        ]
        for copy in copies:
            copy.start()
        return copies

    def stencil(v, k, turn):
        low, high = 2 * turn, 2 * turn + 1
        xlo = jnp.where(x == 0, 0.0, rows_in[low, k : k + 1, :])
        xhi = jnp.where(x == nx - 1, 0.0, rows_in[high, k : k + 1, :])
        wlo = jnp.where(w == 0, 0.0, cols_in[low][:, k : k + 1])
        whi = jnp.where(w == nw - 1, 0.0, cols_in[high][:, k : k + 1])
        return tendency(v, xlo, xhi, wlo, whi, drift[0], drift[1])

    copies = trade(0)
    for copy in copies:
        copy.wait()
    for k in range(3):
        v = gas[k]
        first = v + TIME_STEP * stencil(v, k, 0)
        one[k] = first
        pack(first, k, 1)
    copies = trade(1)
    for copy in copies:
        copy.wait()
    for k in range(3):
        v = one[k]
        two = 0.5 * (gas[k] + v + TIME_STEP * stencil(v, k, 1))
        out[k] = two
        for j in range(per_row):
            table[k, pl.ds(j, rows, stride=per_row), :] = two[:, j * LANES : (j + 1) * LANES]


def gather_kernel(table, tiles, sent):
    count = table.shape[1]
    slots = tiles.shape[0]
    one_hot = (
        tiles[...] == lax.broadcasted_iota(jnp.int32, (slots, count), 1)
    ).astype(F32).astype(BF)
    for k in range(3):
        sent[:, k * LANES : (k + 1) * LANES] = select_rows(one_hot, table[k])


def combine_kernel(got, rate_sums, state_sums, sent):
    sent[...] = got[...] * rate_sums[...] - state_sums[...]


def contact_kernel(pairs, particles, contact, acc, parts):
    step = pl.program_id(0)
    group = contact.shape[0]

    @pl.when(step == 0)
    def _():
        acc[...] = jnp.zeros_like(acc)
        parts[...] = jnp.ones_like(parts)
        for k in range(3):
            high, low = split(particles[:, k, :])
            parts[:, k, :] = high.astype(F32)
            parts[:, k + 3, :] = low.astype(F32)

    for r in range(group):
        at = (step * group + r) * 2
        a, b = pairs[at], pairs[at + 1]
        weight = contact[r].astype(F32).astype(BF)
        part_a, part_b = parts[a], parts[b]
        gain_a = dot(part_b.astype(BF), weight, NT)
        gain_b = dot(part_a.astype(BF), weight, NN)
        acc[a] = acc[a] + (gain_a - gain_a[6:7] * part_a)
        acc[b] = acc[b] + (gain_b - gain_b[6:7] * part_b)


def sums_kernel(slot_row, cells, particles, rates, rate_sums, state_sums, parts, spread):
    slots = rate_sums.shape[0]
    blocks = cells.shape[0]
    parts[...] = jnp.zeros_like(parts)
    for k in range(5):
        value = rates[:, k, :] if k < 2 else rates[:, (k - 2) // 2, :] * particles[:, k - 2, :]
        high, low = split(value)
        parts[:, k, :] = high.astype(F32)
        parts[:, k + 8, :] = low.astype(F32)
    lane_of = lax.broadcasted_iota(jnp.int32, (LANES, LANES), 0)

    def one_group(step, carry):
        base = pl.multiple_of(step * 8, 8)
        near = jnp.bitwise_and(cells[pl.ds(base, 8), :], LANES - 1)
        for r in range(8):
            match = (near[r : r + 1] == lane_of).astype(F32).astype(BF)
            summed = dot(parts[base + r].astype(BF), match, NT)
            spread[base + r] = summed[0:8] + summed[8:16]
        return carry

    lax.fori_loop(0, blocks // 8, one_group, 0)
    into = (
        slot_row[...] == lax.broadcasted_iota(jnp.int32, (slots, blocks), 0)
    ).astype(F32).astype(BF)
    for k in range(5):
        moved = select_rows(into, spread[:, k, :])
        if k == 0:
            rate_sums[:, 0:LANES] = moved
            rate_sums[:, LANES : 2 * LANES] = moved
        elif k == 1:
            rate_sums[:, 2 * LANES : 3 * LANES] = moved
        else:
            state_sums[:, (k - 2) * LANES : (k - 1) * LANES] = moved


def particles_kernel(got, slot_col, cells, particles, rates, acc, out):
    slots = got.shape[0]
    blocks = cells.shape[0]
    one_hot = (
        slot_col[...] == lax.broadcasted_iota(jnp.int32, (blocks, slots), 1)
    ).astype(F32).astype(BF)
    offsets = jnp.bitwise_and(cells[...], LANES - 1)
    for k in range(3):
        tile = select_rows(one_hot, got[:, k * LANES : (k + 1) * LANES])
        picked = jnp.take_along_axis(tile, offsets, axis=1)
        state = particles[:, k, :]
        term = rates[:, k // 2, :] * (picked - state)
        force = DAMPING * (acc[:, k, :] + acc[:, k + 3, :])
        out[:, k, :] = state + TIME_STEP * (term + force)


def sources_kernel(got, tiles, two, out, sums):
    _, rows, cols = two.shape
    per_row = cols // LANES
    slots = got.shape[0]
    count = sums.shape[1]
    one_hot = (
        tiles[...] == lax.broadcasted_iota(jnp.int32, (count, slots), 0)
    ).astype(F32).astype(BF)
    for k in range(3):
        sums[k] = select_rows(one_hot, got[:, k * LANES : (k + 1) * LANES])
        for j in range(per_row):
            cols_j = slice(j * LANES, (j + 1) * LANES)
            out[k, :, cols_j] = two[k, :, cols_j] - (TIME_STEP * LOADING) * sums[
                k, pl.ds(j, rows, stride=per_row), :
            ]


def params():
    return pltpu.CompilerParams(vmem_limit_bytes=VMEM_BYTES)


def cost(flops, moved):
    return pl.CostEstimate(flops=flops, bytes_accessed=moved, transcendentals=0)


def exchange(x):
    return lax.all_to_all(x, ("slab", "pblk"), split_axis=0, concat_axis=0, tiled=True)


def on_device(gas, drift, particles, rates, owner, cells, pairs, contact):
    devices = lax.axis_size("slab") * lax.axis_size("pblk")
    blocks = cells.shape[0]
    depth = max(2, 2 * blocks // devices)
    slots = devices * depth
    tile_count = gas.shape[1] * gas.shape[2] // LANES
    target = owner[:, 0]
    before = jnp.arange(blocks)[None, :] < jnp.arange(blocks)[:, None]
    same = target[None, :] == target[:, None]
    position = jnp.sum((before & same).astype(jnp.int32), axis=1)
    slot = target * depth + position
    tile = cells[:, 0] // LANES
    asked = jnp.sum(
        jnp.where(slot[None, :] == jnp.arange(slots)[:, None], tile[None, :], 0), axis=1
    ).reshape(devices, depth)
    tiles = exchange(asked).reshape(slots)

    field = jax.ShapeDtypeStruct(gas.shape, F32)
    wide = jax.ShapeDtypeStruct((slots, 3 * LANES), F32)
    rows, cols = gas.shape[1:]
    two, table = pl.pallas_call(
        transport_kernel,
        out_shape=(field, jax.ShapeDtypeStruct((3, tile_count, LANES), F32)),
        in_specs=[pl.BlockSpec(memory_space=pltpu.VMEM)] * 2,
        out_specs=(pl.BlockSpec(memory_space=pltpu.VMEM),) * 2,
        scratch_shapes=[
            pltpu.VMEM((3, rows, cols), F32),
            pltpu.VMEM((4, 8, cols), F32),
            pltpu.VMEM((4, rows, LANES), F32),
            pltpu.VMEM((4, 8, cols), F32),
            pltpu.VMEM((4, rows, LANES), F32),
            pltpu.SemaphoreType.DMA((8,)),
            pltpu.SemaphoreType.DMA((8,)),
        ],
        compiler_params=pltpu.CompilerParams(
            collective_id=0, has_side_effects=True, vmem_limit_bytes=VMEM_BYTES
        ),
        cost_estimate=cost(3 * 40 * rows * cols, 30_000_000),
    )(gas, drift)
    sent_gas = pl.pallas_call(gather_kernel, out_shape=wide, compiler_params=params())(
        table, tiles[:, None]
    )
    slot_row, sent_gas = lax.optimization_barrier((slot[None, :], sent_gas))
    rate_sums, state_sums = pl.pallas_call(
        sums_kernel,
        out_shape=(wide, wide),
        scratch_shapes=[pltpu.VMEM((blocks, 16, LANES), F32), pltpu.VMEM((blocks, 8, LANES), F32)],
        compiler_params=params(),
        cost_estimate=cost(blocks * 32 * LANES * LANES, 80_000_000),
    )(slot_row, cells, particles, rates)
    got_gas = exchange(sent_gas)
    sent_terms = pl.pallas_call(combine_kernel, out_shape=wide, compiler_params=params())(
        got_gas, rate_sums, state_sums
    )
    pairs, sent_terms = lax.optimization_barrier((pairs, sent_terms))
    got_terms = exchange(sent_terms)

    pair_count = contact.shape[0]
    group = 8
    acc = pl.pallas_call(
        contact_kernel,
        grid_spec=pltpu.PrefetchScalarGridSpec(
            num_scalar_prefetch=1,
            grid=(pair_count // group,),
            in_specs=[
                pl.BlockSpec(particles.shape, lambda i, s: (0, 0, 0)),
                pl.BlockSpec((group, LANES, LANES), lambda i, s: (i, 0, 0)),
            ],
            out_specs=pl.BlockSpec((blocks, 8, LANES), lambda i, s: (0, 0, 0)),
            scratch_shapes=[pltpu.VMEM((blocks, 8, LANES), F32)],
        ),
        out_shape=jax.ShapeDtypeStruct((blocks, 8, LANES), F32),
        compiler_params=params(),
        cost_estimate=cost(pair_count * 4 * 8 * LANES * LANES, 3 * contact.size * 4),
    )(pairs.reshape(-1), particles, contact)

    particles_next = pl.pallas_call(
        particles_kernel,
        out_shape=jax.ShapeDtypeStruct(particles.shape, F32),
        compiler_params=params(),
        cost_estimate=cost(blocks * slots * 12 * LANES, 10_000_000),
    )(got_gas, slot[:, None], cells, particles, rates, acc)
    gas_next = pl.pallas_call(
        sources_kernel,
        out_shape=field,
        scratch_shapes=[pltpu.VMEM((3, tile_count, LANES), F32)],
        compiler_params=params(),
    )(got_terms, tiles[None, :], two)
    return gas_next, particles_next


def solution(mesh):
    own = ("slab", "pblk")
    grid = P(None, "slab", "pblk")
    in_specs = (
        grid,
        grid,
        P(own, None, None),
        P(own, None, None),
        P(own, None),
        P(own, None),
        P(own, None),
        P(own, None, None),
    )
    return jax.shard_map(
        on_device,
        mesh=mesh,
        in_specs=in_specs,
        out_specs=(grid, P(own, None, None)),
        check_vma=False,
    )
```

```python
import jax
import jax.numpy as jnp
from jax import lax
from jax.experimental import pallas as pl
from jax.experimental.pallas import tpu as pltpu
from jax.sharding import PartitionSpec as P

TIME_STEP = 0.2
VISCOSITY = 0.25
LOADING = 0.5
DAMPING = 0.1
LANES = 128
VMEM_BYTES = 48 * 1024 * 1024
BF = jnp.bfloat16
F32 = jnp.float32
NT = (((1,), (1,)), ((), ()))
NN = (((1,), (0,)), ((), ()))


def dot(a, b, dims=NN):
    return lax.dot_general(a, b, dims, preferred_element_type=F32)


def split(x):
    high = x.astype(BF)
    return high, (x - high.astype(F32)).astype(BF)


def select_rows(one_hot, values):
    high, low = split(values)
    width = values.shape[1]
    both = dot(one_hot, jnp.concatenate([high, low], axis=1))
    return both[:, :width] + both[:, width:]


def tendency(v, xlo, xhi, wlo, whi, drift_x, drift_w):
    rows, cols = v.shape
    row = lax.broadcasted_iota(jnp.int32, v.shape, 0)
    col = lax.broadcasted_iota(jnp.int32, v.shape, 1)
    west = jnp.where(row == 0, xlo, pltpu.roll(v, 1, 0))
    east = jnp.where(row == rows - 1, xhi, pltpu.roll(v, rows - 1, 0))
    south = jnp.where(col == 0, wlo, pltpu.roll(v, 1, 1))
    north = jnp.where(col == cols - 1, whi, pltpu.roll(v, cols - 1, 1))
    upwind = drift_x * (v - west) + drift_w * (v - south)
    return VISCOSITY * (west + east + south + north - 4.0 * v) - upwind


def transport_kernel(
    gas, drift, out, table, one, rows_out, cols_out, rows_in, cols_in, send, recv
):
    _, rows, cols = gas.shape
    per_row = cols // LANES
    x, w = lax.axis_index("slab"), lax.axis_index("pblk")
    nx, nw = lax.axis_size("slab"), lax.axis_size("pblk")
    places = (
        (lax.rem(x + 1, nx), w),
        (lax.rem(x + nx - 1, nx), w),
        (x, lax.rem(w + 1, nw)),
        (x, lax.rem(w + nw - 1, nw)),
    )
    barrier = pltpu.get_barrier_semaphore()
    for place in places:
        pl.semaphore_signal(
            barrier, inc=1, device_id=place, device_id_type=pl.DeviceIdType.MESH
        )
    rows_out[...] = jnp.zeros_like(rows_out)
    cols_out[...] = jnp.zeros_like(cols_out)

    def pack(v, k, turn):
        rows_out[2 * turn, k : k + 1, :] = v[rows - 1 : rows, :]
        rows_out[2 * turn + 1, k : k + 1, :] = v[0:1, :]
        cols_out[2 * turn, :, k : k + 1] = v[:, cols - 1 : cols]
        cols_out[2 * turn + 1, :, k : k + 1] = v[:, 0:1]

    for k in range(3):
        pack(gas[k], k, 0)
    pl.semaphore_wait(barrier, 4)

    def trade(turn):
        low, high = 2 * turn, 2 * turn + 1
        edges = (
            (rows_out.at[low], rows_in.at[low]),
            (rows_out.at[high], rows_in.at[high]),
            (cols_out.at[low], cols_in.at[low]),
            (cols_out.at[high], cols_in.at[high]),
        )
        copies = [
            pltpu.make_async_remote_copy(
                src_ref=src,
                dst_ref=dst,
                send_sem=send.at[4 * turn + n],
                recv_sem=recv.at[4 * turn + n],
                device_id=places[n],
                device_id_type=pl.DeviceIdType.MESH,
            )
            for n, (src, dst) in enumerate(edges)
        ]
        for copy in copies:
            copy.start()
        return copies

    def stencil(v, k, turn):
        low, high = 2 * turn, 2 * turn + 1
        xlo = jnp.where(x == 0, 0.0, rows_in[low, k : k + 1, :])
        xhi = jnp.where(x == nx - 1, 0.0, rows_in[high, k : k + 1, :])
        wlo = jnp.where(w == 0, 0.0, cols_in[low][:, k : k + 1])
        whi = jnp.where(w == nw - 1, 0.0, cols_in[high][:, k : k + 1])
        return tendency(v, xlo, xhi, wlo, whi, drift[0], drift[1])

    copies = trade(0)
    for copy in copies:
        copy.wait()
    for k in range(3):
        v = gas[k]
        first = v + TIME_STEP * stencil(v, k, 0)
        one[k] = first
        pack(first, k, 1)
    copies = trade(1)
    for copy in copies:
        copy.wait()
    for k in range(3):
        v = one[k]
        two = 0.5 * (gas[k] + v + TIME_STEP * stencil(v, k, 1))
        out[k] = two
        for j in range(per_row):
            table[k, pl.ds(j, rows, stride=per_row), :] = two[:, j * LANES : (j + 1) * LANES]


def gather_kernel(table, tiles, sent):
    count = table.shape[1]
    slots = tiles.shape[0]
    one_hot = (
        tiles[...] == lax.broadcasted_iota(jnp.int32, (slots, count), 1)
    ).astype(F32).astype(BF)
    for k in range(3):
        sent[:, k * LANES : (k + 1) * LANES] = select_rows(one_hot, table[k])


def combine_kernel(got, rate_sums, state_sums, sent):
    sent[...] = got[...] * rate_sums[...] - state_sums[...]


def contact_kernel(pairs, particles, contact, acc, parts):
    step = pl.program_id(0)
    group = contact.shape[0]

    @pl.when(step == 0)
    def _():
        acc[...] = jnp.zeros_like(acc)
        parts[...] = jnp.ones_like(parts)
        for k in range(3):
            high, low = split(particles[:, k, :])
            parts[:, k, :] = high.astype(F32)
            parts[:, k + 3, :] = low.astype(F32)

    for r in range(group):
        at = (step * group + r) * 2
        a, b = pairs[at], pairs[at + 1]
        weight = contact[r].astype(F32).astype(BF)
        part_a, part_b = parts[a], parts[b]
        gain_a = dot(part_b.astype(BF), weight, NT)
        gain_b = dot(part_a.astype(BF), weight, NN)
        acc[a] = acc[a] + (gain_a - gain_a[6:7] * part_a)
        acc[b] = acc[b] + (gain_b - gain_b[6:7] * part_b)


def sums_kernel(slot_row, cells, particles, rates, rate_sums, state_sums, parts, spread):
    slots = rate_sums.shape[0]
    blocks = cells.shape[0]
    parts[...] = jnp.zeros_like(parts)
    for k in range(5):
        value = rates[:, k, :] if k < 2 else rates[:, (k - 2) // 2, :] * particles[:, k - 2, :]
        high, low = split(value)
        parts[:, k, :] = high.astype(F32)
        parts[:, k + 8, :] = low.astype(F32)
    lane_of = lax.broadcasted_iota(jnp.int32, (LANES, LANES), 0)

    def one_group(step, carry):
        base = pl.multiple_of(step * 8, 8)
        near = jnp.bitwise_and(cells[pl.ds(base, 8), :], LANES - 1)
        for r in range(8):
            match = (near[r : r + 1] == lane_of).astype(F32).astype(BF)
            summed = dot(parts[base + r].astype(BF), match, NT)
            spread[base + r] = summed[0:8] + summed[8:16]
        return carry

    lax.fori_loop(0, blocks // 8, one_group, 0)
    into = (
        slot_row[...] == lax.broadcasted_iota(jnp.int32, (slots, blocks), 0)
    ).astype(F32).astype(BF)
    for k in range(5):
        moved = select_rows(into, spread[:, k, :])
        if k == 0:
            rate_sums[:, 0:LANES] = moved
            rate_sums[:, LANES : 2 * LANES] = moved
        elif k == 1:
            rate_sums[:, 2 * LANES : 3 * LANES] = moved
        else:
            state_sums[:, (k - 2) * LANES : (k - 1) * LANES] = moved


def particles_kernel(got, slot_col, cells, particles, rates, acc, out):
    slots = got.shape[0]
    blocks = cells.shape[0]
    one_hot = (
        slot_col[...] == lax.broadcasted_iota(jnp.int32, (blocks, slots), 1)
    ).astype(F32).astype(BF)
    offsets = jnp.bitwise_and(cells[...], LANES - 1)
    for k in range(3):
        tile = select_rows(one_hot, got[:, k * LANES : (k + 1) * LANES])
        picked = jnp.take_along_axis(tile, offsets, axis=1)
        state = particles[:, k, :]
        term = rates[:, k // 2, :] * (picked - state)
        force = DAMPING * (acc[:, k, :] + acc[:, k + 3, :])
        out[:, k, :] = state + TIME_STEP * (term + force)


def sources_kernel(got, tiles, two, out, sums):
    _, rows, cols = two.shape
    per_row = cols // LANES
    slots = got.shape[0]
    count = sums.shape[1]
    one_hot = (
        tiles[...] == lax.broadcasted_iota(jnp.int32, (count, slots), 0)
    ).astype(F32).astype(BF)
    for k in range(3):
        sums[k] = select_rows(one_hot, got[:, k * LANES : (k + 1) * LANES])
        for j in range(per_row):
            cols_j = slice(j * LANES, (j + 1) * LANES)
            out[k, :, cols_j] = two[k, :, cols_j] - (TIME_STEP * LOADING) * sums[
                k, pl.ds(j, rows, stride=per_row), :
            ]


def params():
    return pltpu.CompilerParams(vmem_limit_bytes=VMEM_BYTES)


def cost(flops, moved):
    return pl.CostEstimate(flops=flops, bytes_accessed=moved, transcendentals=0)


def exchange(x):
    return lax.all_to_all(x, ("slab", "pblk"), split_axis=0, concat_axis=0, tiled=True)


def on_device(gas, drift, particles, rates, owner, cells, pairs, contact):
    devices = lax.axis_size("slab") * lax.axis_size("pblk")
    blocks = cells.shape[0]
    depth = max(2, 2 * blocks // devices)
    slots = devices * depth
    tile_count = gas.shape[1] * gas.shape[2] // LANES
    target = owner[:, 0]
    before = jnp.arange(blocks)[None, :] < jnp.arange(blocks)[:, None]
    same = target[None, :] == target[:, None]
    position = jnp.sum((before & same).astype(jnp.int32), axis=1)
    slot = target * depth + position
    tile = cells[:, 0] // LANES
    asked = jnp.sum(
        jnp.where(slot[None, :] == jnp.arange(slots)[:, None], tile[None, :], 0), axis=1
    ).reshape(devices, depth)
    tiles = exchange(asked).reshape(slots)

    field = jax.ShapeDtypeStruct(gas.shape, F32)
    wide = jax.ShapeDtypeStruct((slots, 3 * LANES), F32)
    rows, cols = gas.shape[1:]
    two, table = pl.pallas_call(
        transport_kernel,
        out_shape=(field, jax.ShapeDtypeStruct((3, tile_count, LANES), F32)),
        in_specs=[pl.BlockSpec(memory_space=pltpu.VMEM)] * 2,
        out_specs=(pl.BlockSpec(memory_space=pltpu.VMEM),) * 2,
        scratch_shapes=[
            pltpu.VMEM((3, rows, cols), F32),
            pltpu.VMEM((4, 8, cols), F32),
            pltpu.VMEM((4, rows, LANES), F32),
            pltpu.VMEM((4, 8, cols), F32),
            pltpu.VMEM((4, rows, LANES), F32),
            pltpu.SemaphoreType.DMA((8,)),
            pltpu.SemaphoreType.DMA((8,)),
        ],
        compiler_params=pltpu.CompilerParams(
            collective_id=0, has_side_effects=True, vmem_limit_bytes=VMEM_BYTES
        ),
        cost_estimate=cost(3 * 40 * rows * cols, 30_000_000),
    )(gas, drift)
    sent_gas = pl.pallas_call(gather_kernel, out_shape=wide, compiler_params=params())(
        table, tiles[:, None]
    )
    slot_row, sent_gas = lax.optimization_barrier((slot[None, :], sent_gas))
    rate_sums, state_sums = pl.pallas_call(
        sums_kernel,
        out_shape=(wide, wide),
        scratch_shapes=[pltpu.VMEM((blocks, 16, LANES), F32), pltpu.VMEM((blocks, 8, LANES), F32)],
        compiler_params=params(),
        cost_estimate=cost(blocks * 32 * LANES * LANES, 80_000_000),
    )(slot_row, cells, particles, rates)
    got_gas = exchange(sent_gas)
    sent_terms = pl.pallas_call(combine_kernel, out_shape=wide, compiler_params=params())(
        got_gas, rate_sums, state_sums
    )
    pairs, sent_terms = lax.optimization_barrier((pairs, sent_terms))
    got_terms = exchange(sent_terms)

    pair_count = contact.shape[0]
    group = 8
    acc = pl.pallas_call(
        contact_kernel,
        grid_spec=pltpu.PrefetchScalarGridSpec(
            num_scalar_prefetch=1,
            grid=(pair_count // group,),
            in_specs=[
                pl.BlockSpec(particles.shape, lambda i, s: (0, 0, 0)),
                pl.BlockSpec((group, LANES, LANES), lambda i, s: (i, 0, 0)),
            ],
            out_specs=pl.BlockSpec((blocks, 8, LANES), lambda i, s: (0, 0, 0)),
            scratch_shapes=[pltpu.VMEM((blocks, 8, LANES), F32)],
        ),
        out_shape=jax.ShapeDtypeStruct((blocks, 8, LANES), F32),
        compiler_params=params(),
        cost_estimate=cost(pair_count * 4 * 8 * LANES * LANES, 3 * contact.size * 4),
    )(pairs.reshape(-1), particles, contact)

    particles_next = pl.pallas_call(
        particles_kernel,
        out_shape=jax.ShapeDtypeStruct(particles.shape, F32),
        compiler_params=params(),
        cost_estimate=cost(blocks * slots * 12 * LANES, 10_000_000),
    )(got_gas, slot[:, None], cells, particles, rates, acc)
    gas_next = pl.pallas_call(
        sources_kernel,
        out_shape=field,
        scratch_shapes=[pltpu.VMEM((3, tile_count, LANES), F32)],
        compiler_params=params(),
    )(got_terms, tiles[None, :], two)
    return gas_next, particles_next


def solution(mesh):
    own = ("slab", "pblk")
    grid = P(None, "slab", "pblk")
    in_specs = (
        grid,
        grid,
        P(own, None, None),
        P(own, None, None),
        P(own, None),
        P(own, None),
        P(own, None),
        P(own, None, None),
    )
    return jax.shard_map(
        on_device,
        mesh=mesh,
        in_specs=in_specs,
        out_specs=(grid, P(own, None, None)),
        check_vma=False,
    )
```

```python
import jax
import jax.numpy as jnp
from jax import lax
from jax.experimental import pallas as pl
from jax.experimental.pallas import tpu as pltpu
from jax.sharding import PartitionSpec as P

TIME_STEP = 0.2
VISCOSITY = 0.25
LOADING = 0.5
DAMPING = 0.1
LANES = 128
VMEM_BYTES = 48 * 1024 * 1024
BF = jnp.bfloat16
F32 = jnp.float32
NT = (((1,), (1,)), ((), ()))
NN = (((1,), (0,)), ((), ()))


def dot(a, b, dims=NN):
    return lax.dot_general(a, b, dims, preferred_element_type=F32)


def split(x):
    high = x.astype(BF)
    return high, (x - high.astype(F32)).astype(BF)


def select_rows(one_hot, values):
    high, low = split(values)
    width = values.shape[1]
    both = dot(one_hot, jnp.concatenate([high, low], axis=1))
    return both[:, :width] + both[:, width:]


def tendency(v, xlo, xhi, wlo, whi, drift_x, drift_w):
    rows, cols = v.shape
    row = lax.broadcasted_iota(jnp.int32, v.shape, 0)
    col = lax.broadcasted_iota(jnp.int32, v.shape, 1)
    west = jnp.where(row == 0, xlo, pltpu.roll(v, 1, 0))
    east = jnp.where(row == rows - 1, xhi, pltpu.roll(v, rows - 1, 0))
    south = jnp.where(col == 0, wlo, pltpu.roll(v, 1, 1))
    north = jnp.where(col == cols - 1, whi, pltpu.roll(v, cols - 1, 1))
    upwind = drift_x * (v - west) + drift_w * (v - south)
    return VISCOSITY * (west + east + south + north - 4.0 * v) - upwind


def transport_kernel(
    gas, drift, out, table, one, rows_out, cols_out, rows_in, cols_in, send, recv
):
    _, rows, cols = gas.shape
    per_row = cols // LANES
    x, w = lax.axis_index("slab"), lax.axis_index("pblk")
    nx, nw = lax.axis_size("slab"), lax.axis_size("pblk")
    places = (
        (lax.rem(x + 1, nx), w),
        (lax.rem(x + nx - 1, nx), w),
        (x, lax.rem(w + 1, nw)),
        (x, lax.rem(w + nw - 1, nw)),
    )
    barrier = pltpu.get_barrier_semaphore()
    for place in places:
        pl.semaphore_signal(
            barrier, inc=1, device_id=place, device_id_type=pl.DeviceIdType.MESH
        )
    rows_out[...] = jnp.zeros_like(rows_out)
    cols_out[...] = jnp.zeros_like(cols_out)

    def pack(v, k, turn):
        rows_out[2 * turn, k : k + 1, :] = v[rows - 1 : rows, :]
        rows_out[2 * turn + 1, k : k + 1, :] = v[0:1, :]
        cols_out[2 * turn, :, k : k + 1] = v[:, cols - 1 : cols]
        cols_out[2 * turn + 1, :, k : k + 1] = v[:, 0:1]

    for k in range(3):
        pack(gas[k], k, 0)
    pl.semaphore_wait(barrier, 4)

    def trade(turn):
        low, high = 2 * turn, 2 * turn + 1
        edges = (
            (rows_out.at[low], rows_in.at[low]),
            (rows_out.at[high], rows_in.at[high]),
            (cols_out.at[low], cols_in.at[low]),
            (cols_out.at[high], cols_in.at[high]),
        )
        copies = [
            pltpu.make_async_remote_copy(
                src_ref=src,
                dst_ref=dst,
                send_sem=send.at[4 * turn + n],
                recv_sem=recv.at[4 * turn + n],
                device_id=places[n],
                device_id_type=pl.DeviceIdType.MESH,
            )
            for n, (src, dst) in enumerate(edges)
        ]
        for copy in copies:
            copy.start()
        return copies

    def stencil(v, k, turn):
        low, high = 2 * turn, 2 * turn + 1
        xlo = jnp.where(x == 0, 0.0, rows_in[low, k : k + 1, :])
        xhi = jnp.where(x == nx - 1, 0.0, rows_in[high, k : k + 1, :])
        wlo = jnp.where(w == 0, 0.0, cols_in[low][:, k : k + 1])
        whi = jnp.where(w == nw - 1, 0.0, cols_in[high][:, k : k + 1])
        return tendency(v, xlo, xhi, wlo, whi, drift[0], drift[1])

    copies = trade(0)
    for copy in copies:
        copy.wait()
    for k in range(3):
        v = gas[k]
        first = v + TIME_STEP * stencil(v, k, 0)
        one[k] = first
        pack(first, k, 1)
    copies = trade(1)
    for copy in copies:
        copy.wait()
    for k in range(3):
        v = one[k]
        two = 0.5 * (gas[k] + v + TIME_STEP * stencil(v, k, 1))
        out[k] = two
        for j in range(per_row):
            table[k, pl.ds(j, rows, stride=per_row), :] = two[:, j * LANES : (j + 1) * LANES]


def gather_kernel(table, tiles, sent):
    count = table.shape[1]
    slots = tiles.shape[0]
    one_hot = (
        tiles[...] == lax.broadcasted_iota(jnp.int32, (slots, count), 1)
    ).astype(F32).astype(BF)
    for k in range(3):
        sent[:, k * LANES : (k + 1) * LANES] = select_rows(one_hot, table[k])


def combine_kernel(got, rate_sums, state_sums, sent):
    sent[...] = got[...] * rate_sums[...] - state_sums[...]


def contact_kernel(pairs, particles, contact, acc, parts):
    step = pl.program_id(0)
    group = contact.shape[0]

    @pl.when(step == 0)
    def _():
        acc[...] = jnp.zeros_like(acc)
        parts[...] = jnp.ones_like(parts)
        for k in range(3):
            high, low = split(particles[:, k, :])
            parts[:, k, :] = high.astype(F32)
            parts[:, k + 3, :] = low.astype(F32)

    for r in range(group):
        at = (step * group + r) * 2
        a, b = pairs[at], pairs[at + 1]
        weight = contact[r].astype(F32).astype(BF)
        part_a, part_b = parts[a], parts[b]
        gain_a = dot(part_b.astype(BF), weight, NT)
        gain_b = dot(part_a.astype(BF), weight, NN)
        acc[a] = acc[a] + (gain_a - gain_a[6:7] * part_a)
        acc[b] = acc[b] + (gain_b - gain_b[6:7] * part_b)


def sums_kernel(slot_row, cells, particles, rates, rate_sums, state_sums, parts, spread):
    slots = rate_sums.shape[0]
    blocks = cells.shape[0]
    parts[...] = jnp.zeros_like(parts)
    for k in range(5):
        value = rates[:, k, :] if k < 2 else rates[:, (k - 2) // 2, :] * particles[:, k - 2, :]
        high, low = split(value)
        parts[:, k, :] = high.astype(F32)
        parts[:, k + 8, :] = low.astype(F32)
    lane_of = lax.broadcasted_iota(jnp.int32, (LANES, LANES), 0)

    def one_group(step, carry):
        base = pl.multiple_of(step * 8, 8)
        near = jnp.bitwise_and(cells[pl.ds(base, 8), :], LANES - 1)
        for r in range(8):
            match = (near[r : r + 1] == lane_of).astype(F32).astype(BF)
            summed = dot(parts[base + r].astype(BF), match, NT)
            spread[base + r] = summed[0:8] + summed[8:16]
        return carry

    lax.fori_loop(0, blocks // 8, one_group, 0)
    into = (
        slot_row[...] == lax.broadcasted_iota(jnp.int32, (slots, blocks), 0)
    ).astype(F32).astype(BF)
    for k in range(5):
        moved = select_rows(into, spread[:, k, :])
        if k == 0:
            rate_sums[:, 0:LANES] = moved
            rate_sums[:, LANES : 2 * LANES] = moved
        elif k == 1:
            rate_sums[:, 2 * LANES : 3 * LANES] = moved
        else:
            state_sums[:, (k - 2) * LANES : (k - 1) * LANES] = moved


def particles_kernel(got, slot_col, cells, particles, rates, acc, out):
    slots = got.shape[0]
    blocks = cells.shape[0]
    one_hot = (
        slot_col[...] == lax.broadcasted_iota(jnp.int32, (blocks, slots), 1)
    ).astype(F32).astype(BF)
    offsets = jnp.bitwise_and(cells[...], LANES - 1)
    for k in range(3):
        tile = select_rows(one_hot, got[:, k * LANES : (k + 1) * LANES])
        picked = jnp.take_along_axis(tile, offsets, axis=1)
        state = particles[:, k, :]
        term = rates[:, k // 2, :] * (picked - state)
        force = DAMPING * (acc[:, k, :] + acc[:, k + 3, :])
        out[:, k, :] = state + TIME_STEP * (term + force)


def sources_kernel(got, tiles, two, out, sums):
    _, rows, cols = two.shape
    per_row = cols // LANES
    slots = got.shape[0]
    count = sums.shape[1]
    one_hot = (
        tiles[...] == lax.broadcasted_iota(jnp.int32, (count, slots), 0)
    ).astype(F32).astype(BF)
    for k in range(3):
        sums[k] = select_rows(one_hot, got[:, k * LANES : (k + 1) * LANES])
        for j in range(per_row):
            cols_j = slice(j * LANES, (j + 1) * LANES)
            out[k, :, cols_j] = two[k, :, cols_j] - (TIME_STEP * LOADING) * sums[
                k, pl.ds(j, rows, stride=per_row), :
            ]


def params():
    return pltpu.CompilerParams(vmem_limit_bytes=VMEM_BYTES)


def cost(flops, moved):
    return pl.CostEstimate(flops=flops, bytes_accessed=moved, transcendentals=0)


def exchange(x):
    return lax.all_to_all(x, ("slab", "pblk"), split_axis=0, concat_axis=0, tiled=True)


def on_device(gas, drift, particles, rates, owner, cells, pairs, contact):
    devices = lax.axis_size("slab") * lax.axis_size("pblk")
    blocks = cells.shape[0]
    depth = max(2, 2 * blocks // devices)
    slots = devices * depth
    tile_count = gas.shape[1] * gas.shape[2] // LANES
    target = owner[:, 0]
    before = jnp.arange(blocks)[None, :] < jnp.arange(blocks)[:, None]
    same = target[None, :] == target[:, None]
    position = jnp.sum((before & same).astype(jnp.int32), axis=1)
    slot = target * depth + position
    tile = cells[:, 0] // LANES
    asked = jnp.sum(
        jnp.where(slot[None, :] == jnp.arange(slots)[:, None], tile[None, :], 0), axis=1
    ).reshape(devices, depth)
    me = lax.axis_index("slab") * lax.axis_size("pblk") + lax.axis_index("pblk")
    asked_all = lax.all_gather(asked, ("slab", "pblk"))
    tiles = lax.dynamic_index_in_dim(asked_all, me, axis=1, keepdims=False).reshape(slots)

    field = jax.ShapeDtypeStruct(gas.shape, F32)
    wide = jax.ShapeDtypeStruct((slots, 3 * LANES), F32)
    rows, cols = gas.shape[1:]
    two, table = pl.pallas_call(
        transport_kernel,
        out_shape=(field, jax.ShapeDtypeStruct((3, tile_count, LANES), F32)),
        in_specs=[pl.BlockSpec(memory_space=pltpu.VMEM)] * 2,
        out_specs=(pl.BlockSpec(memory_space=pltpu.VMEM),) * 2,
        scratch_shapes=[
            pltpu.VMEM((3, rows, cols), F32),
            pltpu.VMEM((4, 8, cols), F32),
            pltpu.VMEM((4, rows, LANES), F32),
            pltpu.VMEM((4, 8, cols), F32),
            pltpu.VMEM((4, rows, LANES), F32),
            pltpu.SemaphoreType.DMA((8,)),
            pltpu.SemaphoreType.DMA((8,)),
        ],
        compiler_params=pltpu.CompilerParams(
            collective_id=0, has_side_effects=True, vmem_limit_bytes=VMEM_BYTES
        ),
        cost_estimate=cost(3 * 40 * rows * cols, 30_000_000),
    )(gas, drift)
    sent_gas = pl.pallas_call(gather_kernel, out_shape=wide, compiler_params=params())(
        table, tiles[:, None]
    )
    slot_row, sent_gas = lax.optimization_barrier((slot[None, :], sent_gas))
    rate_sums, state_sums = pl.pallas_call(
        sums_kernel,
        out_shape=(wide, wide),
        scratch_shapes=[pltpu.VMEM((blocks, 16, LANES), F32), pltpu.VMEM((blocks, 8, LANES), F32)],
        compiler_params=params(),
        cost_estimate=cost(blocks * 32 * LANES * LANES, 80_000_000),
    )(slot_row, cells, particles, rates)
    got_gas = exchange(sent_gas)
    sent_terms = pl.pallas_call(combine_kernel, out_shape=wide, compiler_params=params())(
        got_gas, rate_sums, state_sums
    )
    pairs, sent_terms = lax.optimization_barrier((pairs, sent_terms))
    got_terms = exchange(sent_terms)

    pair_count = contact.shape[0]
    group = 8
    acc = pl.pallas_call(
        contact_kernel,
        grid_spec=pltpu.PrefetchScalarGridSpec(
            num_scalar_prefetch=1,
            grid=(pair_count // group,),
            in_specs=[
                pl.BlockSpec(particles.shape, lambda i, s: (0, 0, 0)),
                pl.BlockSpec((group, LANES, LANES), lambda i, s: (i, 0, 0)),
            ],
            out_specs=pl.BlockSpec((blocks, 8, LANES), lambda i, s: (0, 0, 0)),
            scratch_shapes=[pltpu.VMEM((blocks, 8, LANES), F32)],
        ),
        out_shape=jax.ShapeDtypeStruct((blocks, 8, LANES), F32),
        compiler_params=params(),
        cost_estimate=cost(pair_count * 4 * 8 * LANES * LANES, 3 * contact.size * 4),
    )(pairs.reshape(-1), particles, contact)

    particles_next = pl.pallas_call(
        particles_kernel,
        out_shape=jax.ShapeDtypeStruct(particles.shape, F32),
        compiler_params=params(),
        cost_estimate=cost(blocks * slots * 12 * LANES, 10_000_000),
    )(got_gas, slot[:, None], cells, particles, rates, acc)
    gas_next = pl.pallas_call(
        sources_kernel,
        out_shape=field,
        scratch_shapes=[pltpu.VMEM((3, tile_count, LANES), F32)],
        compiler_params=params(),
    )(got_terms, tiles[None, :], two)
    return gas_next, particles_next


def solution(mesh):
    own = ("slab", "pblk")
    grid = P(None, "slab", "pblk")
    in_specs = (
        grid,
        grid,
        P(own, None, None),
        P(own, None, None),
        P(own, None),
        P(own, None),
        P(own, None),
        P(own, None, None),
    )
    return jax.shard_map(
        on_device,
        mesh=mesh,
        in_specs=in_specs,
        out_specs=(grid, P(own, None, None)),
        check_vma=False,
    )
```
